128 devices in a mesh: dev: 128 (over x, y, z, core).
Axes of the slice: x: 4, y: 4, z: 4, core: 2. Of those that a mesh axis runs over, the one named last changes fastest.
Arguments:
- collocation: bfloat16 [32768, 16384], P(None, 'dev'), may hold values from -6 to 6
- cholesky_tiles: bfloat16 [2048, 4, 128, 128], P('dev'), may hold values from -0.0029296875 to 0.0029296875
- tile_blocks: int32 [2048, 2], replicated, may hold values from 0 to 255
- tile_lists: int32 [128, 256], P('dev'), may hold values from 0 to 2047, as said below
- list_lengths: int32 [128], P('dev'), may hold values from 85 to 256, as said below
Outputs:
- projected_rhs: float32 [4, 16384], P(None, 'dev')
The draws below stay inside these ranges and needn't reach their ends.
Inputs may be any that keep to these rules, and one draw needn't show every extreme that they name: `tile_lists`: entry s of block d is live when s < list_lengths[d]. The live entries of one block are distinct tile ids, and at most 2 of them name tiles of one owner (device tile_id // 16); the block with the longest list names exactly 2 tiles of every owner, and some owner is named by exactly 2 live entries of every block. Entries past the length count for nothing. `list_lengths`: one block's list is full.
All inputs are finite; a program needn't handle non-finite values.
Results may differ from the reference program's by a relative error of at most 0.0003.
Values may be sent and summed in bfloat16 or wider, within the bound.
No kernel may reach another device: no remote copies, remote signals or barrier semaphores. Data moves between devices by JAX's collectives and lax.ppermute only.
A program may use at most 192 MiB of HBM per device.

```python
import jax
import jax.numpy as jnp
from jax import lax

NB = 128
NAO = 32768
AOB = 256
BP = 128
K = 4
CAP = 2
TILE_DEV = 16
POINT_BLOCKS = 128
SLOTS = 256
NTILES = 2048
NPTS = 16384


def lists_and_lengths(key):
    subkeys = jax.random.split(key, 7)
    slot_index = jnp.arange(SLOTS, dtype=jnp.int32)
    owners = slot_index // CAP
    slot_rank = slot_index % CAP
    first_local = jax.random.randint(subkeys[0], (POINT_BLOCKS, POINT_BLOCKS), 0, TILE_DEV)
    stride = jax.random.randint(subkeys[1], (POINT_BLOCKS, POINT_BLOCKS), 1, TILE_DEV)
    local_ids = (first_local[:, owners] + slot_rank[None, :] * stride[:, owners]) % TILE_DEV
    tile_ids = owners[None, :] * TILE_DEV + local_ids
    full_owner = jax.random.randint(subkeys[2], (), 0, POINT_BLOCKS)
    ranking = jax.random.randint(subkeys[3], (POINT_BLOCKS, SLOTS), 0, 1048576) * SLOTS + slot_index[None, :] + SLOTS
    ranking = jnp.where(owners[None, :] == full_owner, slot_index[None, :], ranking)
    arranged = jnp.take_along_axis(tile_ids, jnp.argsort(ranking, axis=1), axis=1)
    shortest = SLOTS // 3
    rotation = jax.random.randint(subkeys[4], (POINT_BLOCKS, 1), 0, shortest - CAP + 1)
    entry_lists = jnp.take_along_axis(arranged, (slot_index[None, :] - rotation) % SLOTS, axis=1)
    lengths = jax.random.randint(subkeys[5], (POINT_BLOCKS,), shortest, SLOTS + 1)
    longest = jax.random.randint(subkeys[6], (), 0, POINT_BLOCKS)
    lengths = jnp.where(jnp.arange(POINT_BLOCKS) == longest, SLOTS, lengths)
    return (entry_lists.astype(jnp.int32), lengths.astype(jnp.int32))


def draw_tile_lists(key, part):
    entry_lists, lengths = lists_and_lengths(key)
    return entry_lists


def draw_list_lengths(key, part):
    entry_lists, lengths = lists_and_lengths(key)
    return lengths


def plant(values, rng, low, high):
    place = [jax.random.randint(jax.random.fold_in(rng, axis), (), 0, length) for axis, length in enumerate(values.shape)]
    widest = values.shape.index(max(values.shape))
    next_to = place[:widest] + [(place[widest] + 1) % values.shape[widest]] + place[widest + 1:]
    return values.at[tuple(place)].set(low).at[tuple(next_to)].set(high)


def block_scale(rng, dims, shards, least, largest):
    def one(dim, shards_of):
        steps = jax.random.uniform(jax.random.fold_in(jax.random.fold_in(rng, 6), dim), (shards_of,), jnp.float32, least / len(shards), largest / len(shards))
        return jnp.repeat(jnp.exp(steps), dims[dim] // shards_of).reshape((-1,) + (1,) * (len(dims) - dim - 1))

    factor_of = one(*shards[0])
    for cut in shards[1:]:
        factor_of = factor_of * one(*cut)
    return factor_of


def centred(own_key, dims, deviation, limit, pieces=(), held_as=jnp.bfloat16):
    result = deviation * jax.random.normal(own_key, dims, jnp.float32)
    if pieces:
        result = result * block_scale(own_key, dims, pieces, -0.22, 0.18)
    return jnp.clip(result, -limit, limit).astype(held_as)


def setup_inputs(seed: int = 0) -> dict:
    key_of = jax.random.split(jax.random.key(seed), 6)
    collocation = centred(key_of[0], (NAO, NPTS), 1.0, 6.0, ((1, 128),))
    cholesky_tiles = centred(key_of[1], (NTILES, K, NB, NB), (NB * NB * SLOTS) ** -0.5, 0.0029296875, ((0, 128),))
    tile_blocks = plant(jax.random.randint(key_of[2], (NTILES, 2), 0, AOB), jax.random.fold_in(key_of[2], 1), 0, AOB - 1).astype(jnp.int32)
    tile_lists = draw_tile_lists(jax.random.fold_in(key_of[5], 71), 0)
    list_lengths = draw_list_lengths(jax.random.fold_in(key_of[5], 71), 0)
    return dict(collocation=collocation, cholesky_tiles=cholesky_tiles, tile_blocks=tile_blocks, tile_lists=tile_lists, list_lengths=list_lengths)


batch_entries = 16


def entry_terms(tiles, left_rows, right_rows):
    products = jnp.einsum("tkab,tbp->tkap", tiles.astype(jnp.float32), right_rows.astype(jnp.float32))
    return jnp.sum(products * left_rows.astype(jnp.float32)[:, None, :, :], axis=2)


def reference(collocation, cholesky_tiles, tile_blocks, tile_lists, list_lengths):
    def block_rhs(block_index):
        local_points = lax.dynamic_slice_in_dim(collocation, block_index * BP, BP, 1).reshape(AOB, NB, BP)
        entries = tile_lists[block_index]
        length = list_lengths[block_index]

        def add_block(turn_index, totals):
            offset = turn_index * batch_entries
            chosen = lax.dynamic_slice_in_dim(entries, offset, batch_entries)
            valid = (offset + jnp.arange(batch_entries, dtype=jnp.int32)) < length
            block_pairs = tile_blocks[chosen]
            terms = entry_terms(cholesky_tiles[chosen], local_points[block_pairs[:, 0]], local_points[block_pairs[:, 1]])
            terms = jnp.where(valid[:, None, None], terms, 0.0)
            return totals + jnp.sum(terms, axis=0)

        turns = (length + batch_entries - 1) // batch_entries
        return lax.fori_loop(0, turns, add_block, jnp.zeros((K, BP), jnp.float32))

    stacked_rhs = lax.map(block_rhs, jnp.arange(POINT_BLOCKS, dtype=jnp.int32))
    return jnp.transpose(stacked_rhs, (1, 0, 2)).reshape(K, POINT_BLOCKS * BP)
```

```python
import functools

import jax
import jax.numpy as jnp
from jax import lax
from jax.experimental import pallas as pl
from jax.experimental.pallas import tpu as pltpu
from jax.sharding import PartitionSpec as P

step_blocks = 16


def pick_kernel(ids_ref, rows_ref, out_ref, sem):
    owners = out_ref.shape[0]

    def send(o, carry):
        pltpu.make_async_copy(rows_ref.at[ids_ref[0, o]], out_ref.at[o, 0], sem).start()
        pltpu.make_async_copy(rows_ref.at[ids_ref[1, o]], out_ref.at[o, 1], sem).start()
        return carry

    lax.fori_loop(0, owners, send, 0)
    pltpu.make_async_copy(out_ref, out_ref, sem).wait()


def pick_rows(row_blocks, ids):
    owners = ids.shape[1]
    edge, points = row_blocks.shape[1:]
    return pl.pallas_call(
        pick_kernel,
        out_shape=jax.ShapeDtypeStruct((owners, 2, edge, points), row_blocks.dtype),
        in_specs=[
            pl.BlockSpec(memory_space=pltpu.SMEM),
            pl.BlockSpec(memory_space=pltpu.VMEM),
        ],
        out_specs=pl.BlockSpec(memory_space=pl.ANY),
        scratch_shapes=[pltpu.SemaphoreType.DMA],
        compiler_params=pltpu.CompilerParams(vmem_limit_bytes=24 * 2**20),
    )(ids, row_blocks)


def terms_kernel(ids_ref, tiles_ref, pairs_ref, before_ref, out_ref):
    blocks = pairs_ref.shape[0]
    vectors, edge = tiles_ref.shape[1:3]
    points = pairs_ref.shape[3]
    base = pl.program_id(0) * blocks
    for i in range(blocks):
        tile_id = ids_ref[base + i]
        tile = tiles_ref[jnp.maximum(tile_id, 0)].reshape(vectors * edge, edge)
        left = pairs_ref[i, 0].astype(jnp.float32)
        product = jnp.dot(tile, pairs_ref[i, 1], preferred_element_type=jnp.float32)
        term = jnp.sum(product.reshape(vectors, edge, points) * left[None], axis=1)
        out_ref[i] = before_ref[i] + jnp.where(tile_id >= 0, term, 0.0)


def add_terms(ids, tiles, pairs, before):
    count, _, edge, points = pairs.shape
    owned, vectors = tiles.shape[:2]
    return pl.pallas_call(
        terms_kernel,
        out_shape=jax.ShapeDtypeStruct((count, vectors, points), jnp.float32),
        grid_spec=pltpu.PrefetchScalarGridSpec(
            num_scalar_prefetch=1,
            grid=(count // step_blocks,),
            in_specs=[
                pl.BlockSpec((owned, vectors, edge, edge), lambda g, ids: (0, 0, 0, 0)),
                pl.BlockSpec((step_blocks, 2, edge, points), lambda g, ids: (g, 0, 0, 0)),
                pl.BlockSpec((step_blocks, vectors, points), lambda g, ids: (g, 0, 0)),
            ],
            out_specs=pl.BlockSpec((step_blocks, vectors, points), lambda g, ids: (g, 0, 0)),
        ),
        compiler_params=pltpu.CompilerParams(vmem_limit_bytes=24 * 2**20),
        cost_estimate=pl.CostEstimate(
            flops=2 * count * vectors * edge * edge * points,
            bytes_accessed=count * 2 * edge * points * 2,
            transcendentals=0,
        ),
    )(ids, tiles, pairs, before)


def local(collocation, cholesky_tiles, tile_blocks, tile_lists, list_lengths):
    basis_count, points = collocation.shape
    owned_count, vectors, edge = cholesky_tiles.shape[:3]
    devices = lax.axis_size("dev")
    me = lax.axis_index("dev")
    row_blocks = collocation.reshape(basis_count // edge, edge, points)
    entries = tile_lists[0]
    live = jnp.arange(entries.shape[0], dtype=jnp.int32) < list_lengths[0]
    named = live[None, :] & (
        entries[None, :] // owned_count == jnp.arange(devices, dtype=jnp.int32)[:, None]
    )
    last = jnp.max(jnp.where(named, entries[None, :], -1), axis=1)
    first = jnp.min(jnp.where(named, entries[None, :], devices * owned_count), axis=1)
    slots = jnp.stack([last, jnp.where(first < last, first, -1)])
    all_slots = lax.all_gather(slots, "dev")
    pair_ids = tile_blocks[jnp.maximum(slots, 0)]
    sent = [pick_rows(row_blocks, pair_ids[r].T) for r in range(2)]
    arrived = [lax.all_to_all(s, "dev", split_axis=0, concat_axis=0, tiled=True) for s in sent]
    mine = lax.dynamic_slice_in_dim(all_slots, me, 1, 2)[:, :, 0]
    mine = jnp.where(mine >= 0, mine - me * owned_count, -1)
    partial = jnp.zeros((devices, vectors, points), jnp.float32)
    for r in range(2):
        partial = add_terms(mine[:, r], cholesky_tiles, arrived[r], partial)
    returned = lax.all_to_all(partial, "dev", split_axis=0, concat_axis=0, tiled=True)
    return jnp.sum(returned, axis=0)


def solution(mesh):
    return jax.shard_map(
        local,
        mesh=mesh,
        in_specs=(P(None, "dev"), P("dev", None, None, None), P(), P("dev", None), P("dev")),
        out_specs=P(None, "dev"),
        check_vma=False,
    )
```

```python
import jax
import jax.numpy as jnp
from jax import lax
from jax.experimental import pallas as pl
from jax.experimental.pallas import tpu as pltpu
from jax.sharding import PartitionSpec as P

cores = 2
capacity = 4
sublanes = 8
id_rows = 16
chips_per_turn = 4
sources_per_fetch = 8


def pick_kernel(
    length_ref, list_ref, pairs_ref, rows_hbm, out_hbm, rows, staged, slots, filled, fetch_sem, sems
):
    edge = rows.shape[1]
    chips = filled.shape[0]
    chip_tiles = pairs_ref.shape[1] // chips
    turns = chips // chips_per_turn
    fetch = pltpu.make_async_copy(rows_hbm, rows, fetch_sem)
    fetch.start()

    def clear(q, carry):
        filled[q] = 0
        for r in range(capacity):
            slots[q * capacity + r] = -1
        return carry

    lax.fori_loop(0, chips, clear, 0)

    def enter(s, carry):
        tile = list_ref[0, s]
        chip = tile // chip_tiles
        rank = filled[chip]
        slots[chip * capacity + rank] = tile
        filled[chip] = rank + 1
        return carry

    lax.fori_loop(0, length_ref[0], enter, 0)
    fetch.wait()
    lane = lax.broadcasted_iota(jnp.int32, (id_rows, edge), 1)

    def store(g):
        part = pl.ds(g * chips_per_turn, chips_per_turn)
        return pltpu.make_async_copy(staged.at[part], out_hbm.at[part], sems.at[g])

    def fill(g, carry):
        for i in range(chips_per_turn):
            chip = g * chips_per_turn + i
            ids = jnp.zeros((id_rows, edge), jnp.int32)
            for r in range(capacity):
                tile = slots[chip * capacity + r]
                known = jnp.maximum(tile, 0)
                for side in range(2):
                    at = (2 * r + side) * edge
                    staged[chip, at : at + edge, :] = rows[pairs_ref[side, known]]
                ids = jnp.where(lane == r, jnp.where(tile >= 0, tile % chip_tiles + 1, 0), ids)
            top = 2 * capacity * edge
            staged[chip, top : top + id_rows, :] = ids.astype(jnp.float32).astype(staged.dtype)
        store(g).start()
        return carry

    lax.fori_loop(0, turns, fill, 0)

    def finish(g, carry):
        store(g).wait()
        return carry

    lax.fori_loop(0, turns, finish, 0)


def pick_rows(length, entries, pairs, row_blocks, chips):
    blocks, edge, points = row_blocks.shape
    payload = 2 * capacity * edge + id_rows
    return pl.pallas_call(
        pick_kernel,
        out_shape=jax.ShapeDtypeStruct((chips, payload, points), row_blocks.dtype),
        in_specs=[
            pl.BlockSpec(memory_space=pltpu.SMEM),
            pl.BlockSpec(memory_space=pltpu.SMEM),
            pl.BlockSpec(memory_space=pltpu.SMEM),
            pl.BlockSpec(memory_space=pl.ANY),
        ],
        out_specs=pl.BlockSpec(memory_space=pl.ANY),
        scratch_shapes=[
            pltpu.VMEM((blocks, edge, points), row_blocks.dtype),
            pltpu.VMEM((chips, payload, points), row_blocks.dtype),
            pltpu.SMEM((chips * capacity,), jnp.int32),
            pltpu.SMEM((chips,), jnp.int32),
            pltpu.SemaphoreType.DMA,
            pltpu.SemaphoreType.DMA((chips // chips_per_turn,)),
        ],
        compiler_params=pltpu.CompilerParams(vmem_limit_bytes=56 * 2**20),
    )(length, entries, pairs, row_blocks)


def terms_kernel(payload_hbm, own_hbm, other_hbm, out_ref, payload, tiles, ids_vmem, ids_row, ids, sems):
    sources = payload.shape[0]
    owned, vectors, edge = own_hbm.shape[:3]
    points = payload.shape[2]
    fetches = sources // sources_per_fetch
    top = 2 * capacity * edge
    core = lax.rem(lax.axis_index("dev"), cores)
    ids_copy = pltpu.make_async_copy(
        payload_hbm.at[:, pl.ds(top, id_rows), :], ids_vmem, sems.at[fetches]
    )
    own_copy = pltpu.make_async_copy(
        own_hbm, tiles.at[pl.ds(core * owned, owned)], sems.at[fetches + 1]
    )
    other_copy = pltpu.make_async_copy(
        other_hbm, tiles.at[pl.ds((1 - core) * owned, owned)], sems.at[fetches + 2]
    )

    def block_copy(g):
        part = pl.ds(g * sources_per_fetch, sources_per_fetch)
        rows = pl.ds(0, top)
        return pltpu.make_async_copy(payload_hbm.at[part, rows, :], payload.at[part], sems.at[g])

    ids_copy.start()
    own_copy.start()
    other_copy.start()
    for g in range(fetches):
        block_copy(g).start()
    ids_copy.wait()
    for i in range(sources):
        ids_row[i : i + 1, :] = ids_vmem[i].astype(jnp.float32)[0:1, :].astype(jnp.int32)
    pltpu.sync_copy(ids_row, ids)
    own_copy.wait()
    other_copy.wait()

    def one_fetch(g, carry):
        block_copy(g).wait()
        for i in range(sources_per_fetch):
            source = g * sources_per_fetch + i
            total = jnp.zeros((vectors, sublanes, points), jnp.float32)
            for r in range(capacity):
                found = ids[source, r] - 1
                tile = tiles[jnp.maximum(found, 0)].reshape(vectors * edge, edge)
                at = 2 * r * edge
                left = payload[source, at : at + edge, :].astype(jnp.float32)
                right = payload[source, at + edge : at + 2 * edge, :]
                product = jnp.dot(tile, right, preferred_element_type=jnp.float32)
                product = product.reshape(vectors, edge // sublanes, sublanes, points)
                left = left.reshape(1, edge // sublanes, sublanes, points)
                term = jnp.sum(product * left, axis=1)
                total = total + jnp.where(found >= 0, term, 0.0)
            out_ref[source] = jnp.sum(total, axis=1)
        return carry

    lax.fori_loop(0, fetches, one_fetch, 0)


def form_terms(payload, own, other):
    sources, rows, points = payload.shape
    owned, vectors, edge = own.shape[:3]
    top = 2 * capacity * edge
    return pl.pallas_call(
        terms_kernel,
        out_shape=jax.ShapeDtypeStruct((sources, vectors, points), jnp.float32),
        in_specs=[pl.BlockSpec(memory_space=pl.ANY)] * 3,
        out_specs=pl.BlockSpec(memory_space=pltpu.VMEM),
        scratch_shapes=[
            pltpu.VMEM((sources, top, points), payload.dtype),
            pltpu.VMEM((cores * owned, vectors, edge, edge), own.dtype),
            pltpu.VMEM((sources, id_rows, points), payload.dtype),
            pltpu.VMEM((sources, points), jnp.int32),
            pltpu.SMEM((sources, points), jnp.int32),
            pltpu.SemaphoreType.DMA((sources // sources_per_fetch + 3,)),
        ],
        compiler_params=pltpu.CompilerParams(vmem_limit_bytes=56 * 2**20),
    )(payload, own, other)


def local(collocation, cholesky_tiles, tile_blocks, tile_lists, list_lengths):
    basis_count, points = collocation.shape
    edge = cholesky_tiles.shape[2]
    devices = lax.axis_size("dev")
    chips = devices // cores
    same_core = [[q * cores + c for q in range(chips)] for c in range(cores)]
    swap = [(d, d ^ 1) for d in range(devices)]
    other_tiles = lax.ppermute(cholesky_tiles, "dev", swap)
    row_blocks = collocation.reshape(basis_count // edge, edge, points)
    sent = pick_rows(list_lengths, tile_lists, tile_blocks.T, row_blocks, chips)
    sent, other_tiles = lax.optimization_barrier((sent, other_tiles))
    arrived = lax.all_to_all(
        sent, "dev", split_axis=0, concat_axis=0, tiled=True, axis_index_groups=same_core
    )
    partial = form_terms(arrived, cholesky_tiles, other_tiles)
    returned = lax.all_to_all(
        partial, "dev", split_axis=0, concat_axis=0, tiled=True, axis_index_groups=same_core
    )
    return jnp.sum(returned, axis=0)


def solution(mesh):
    return jax.shard_map(
        local,
        mesh=mesh,
        in_specs=(P(None, "dev"), P("dev", None, None, None), P(), P("dev", None), P("dev")),
        out_specs=P(None, "dev"),
        check_vma=False,
    )
```

```python
import functools

import jax
import jax.numpy as jnp
from jax import lax
from jax.experimental import pallas as pl
from jax.experimental.pallas import tpu as pltpu
from jax.sharding import PartitionSpec as P

cores = 2
per_owner = 2
capacity = cores * per_owner
sublanes = 8
id_rows = 16
chips_per_turn = 4
sources_per_turn = 16


def pick_kernel(
    length_hbm,
    list_hbm,
    pairs_hbm,
    rows_hbm,
    out_hbm,
    rows,
    staged,
    length_ref,
    list_ref,
    pairs_ref,
    slots,
    filled,
    fetch_sems,
    sems,
):
    edge = rows.shape[1]
    chips = staged.shape[0]
    owned = pairs_ref.shape[1] // filled.shape[0]
    turns = chips // chips_per_turn
    length_fetch = pltpu.make_async_copy(length_hbm, length_ref, fetch_sems.at[0])
    list_fetch = pltpu.make_async_copy(list_hbm, list_ref, fetch_sems.at[1])
    pairs_fetch = pltpu.make_async_copy(pairs_hbm, pairs_ref, fetch_sems.at[2])
    fetch = pltpu.make_async_copy(rows_hbm, rows, fetch_sems.at[3])
    length_fetch.start()
    list_fetch.start()
    pairs_fetch.start()
    fetch.start()

    def clear(o, carry):
        filled[o] = 0
        for r in range(per_owner):
            slots[o * per_owner + r] = -1
        return carry

    lax.fori_loop(0, filled.shape[0], clear, 0)
    length_fetch.wait()
    list_fetch.wait()

    def enter(s, carry):
        tile = list_ref[0, s]
        owner = tile // owned
        rank = filled[owner]
        slots[owner * per_owner + rank] = tile
        filled[owner] = rank + 1
        return carry

    lax.fori_loop(0, length_ref[0], enter, 0)
    pairs_fetch.wait()
    fetch.wait()
    lane = lax.broadcasted_iota(jnp.int32, (id_rows, edge), 1)

    def store(g):
        part = pl.ds(g * chips_per_turn, chips_per_turn)
        return pltpu.make_async_copy(staged.at[part], out_hbm.at[part], sems.at[g])

    def fill(g, carry):
        for i in range(chips_per_turn):
            chip = g * chips_per_turn + i
            ids = jnp.zeros((id_rows, edge), jnp.int32)
            for r in range(capacity):
                tile = slots[chip * capacity + r]
                known = jnp.maximum(tile, 0)
                for side in range(2):
                    at = (2 * r + side) * edge
                    staged[chip, at : at + edge, :] = rows[pairs_ref[side, known]]
                ids = jnp.where(lane == r, jnp.where(tile >= 0, tile % owned + 1, 0), ids)
            top = 2 * capacity * edge
            staged[chip, top : top + id_rows, :] = ids.astype(jnp.float32).astype(staged.dtype)
        store(g).start()
        return carry

    lax.fori_loop(0, turns, fill, 0)

    def finish(g, carry):
        store(g).wait()
        return carry

    lax.fori_loop(0, turns, finish, 0)


def pick_rows(length, entries, pairs, row_blocks, chips):
    blocks, edge, points = row_blocks.shape
    payload = 2 * capacity * edge + id_rows
    return pl.pallas_call(
        pick_kernel,
        out_shape=jax.ShapeDtypeStruct((chips, payload, points), row_blocks.dtype),
        in_specs=[pl.BlockSpec(memory_space=pl.ANY)] * 4,
        out_specs=pl.BlockSpec(memory_space=pl.ANY),
        scratch_shapes=[
            pltpu.VMEM((blocks, edge, points), row_blocks.dtype),
            pltpu.VMEM((chips, payload, points), row_blocks.dtype),
            pltpu.SMEM(length.shape, length.dtype),
            pltpu.SMEM(entries.shape, entries.dtype),
            pltpu.SMEM(pairs.shape, pairs.dtype),
            pltpu.SMEM((chips * capacity,), jnp.int32),
            pltpu.SMEM((chips * cores,), jnp.int32),
            pltpu.SemaphoreType.DMA((4,)),
            pltpu.SemaphoreType.DMA((chips // chips_per_turn,)),
        ],
        compiler_params=pltpu.CompilerParams(vmem_limit_bytes=56 * 2**20),
    )(length, entries, pairs, row_blocks)


def terms_kernel(partner, payload, tiles, before, out_ref, ids_row, ids):
    sources, _, points = payload.shape
    vectors, edge = tiles.shape[1:3]
    top = 2 * capacity * edge
    core = lax.rem(lax.axis_index("dev"), cores)
    first = (1 - core if partner else core) * per_owner
    for i in range(sources):
        row = payload[i, top : top + id_rows, :].astype(jnp.float32)[0:1, :]
        ids_row[i : i + 1, :] = row.astype(jnp.int32)
    pltpu.sync_copy(ids_row, ids)

    def one_turn(g, carry):
        for i in range(sources_per_turn):
            source = g * sources_per_turn + i
            total = jnp.zeros((vectors, sublanes, points), jnp.float32)
            for r in range(per_owner):
                slot = first + r
                found = ids[source, slot] - 1
                tile = tiles[jnp.maximum(found, 0)].reshape(vectors * edge, edge)
                at = pl.multiple_of(2 * slot * edge, edge)
                left = payload[source, pl.ds(at, edge), :].astype(jnp.float32)
                right = payload[source, pl.ds(at + edge, edge), :]
                product = jnp.dot(tile, right, preferred_element_type=jnp.float32)
                product = product.reshape(vectors, edge // sublanes, sublanes, points)
                left = left.reshape(1, edge // sublanes, sublanes, points)
                term = jnp.sum(product * left, axis=1)
                total = total + jnp.where(found >= 0, term, 0.0)
            out_ref[source] = before[source] + jnp.sum(total, axis=1)
        return carry

    lax.fori_loop(0, sources // sources_per_turn, one_turn, 0)


def add_terms(partner, payload, tiles, before):
    sources, rows, points = payload.shape
    return pl.pallas_call(
        functools.partial(terms_kernel, partner),
        out_shape=jax.ShapeDtypeStruct(before.shape, before.dtype),
        in_specs=[pl.BlockSpec(memory_space=pltpu.VMEM)] * 3,
        out_specs=pl.BlockSpec(memory_space=pltpu.VMEM),
        scratch_shapes=[
            pltpu.VMEM((sources, points), jnp.int32),
            pltpu.SMEM((sources, points), jnp.int32),
        ],
        compiler_params=pltpu.CompilerParams(vmem_limit_bytes=12 * 2**20),
        cost_estimate=pl.CostEstimate(
            flops=4 * sources * tiles.size // tiles.shape[0] * points,
            bytes_accessed=payload.size,
            transcendentals=0,
        ),
    )(payload, tiles, before)


def local(collocation, cholesky_tiles, tile_blocks, tile_lists, list_lengths):
    basis_count, points = collocation.shape
    vectors, edge = cholesky_tiles.shape[1:3]
    devices = lax.axis_size("dev")
    chips = devices // cores
    same_core = [[q * cores + c for q in range(chips)] for c in range(cores)]
    swap = [(d, d ^ 1) for d in range(devices)]
    row_blocks = collocation.reshape(basis_count // edge, edge, points)
    sent = pick_rows(list_lengths, tile_lists, tile_blocks.T, row_blocks, chips)
    arrived = lax.all_to_all(
        sent, "dev", split_axis=0, concat_axis=0, tiled=True, axis_index_groups=same_core
    )
    _, own_tiles = lax.optimization_barrier((arrived, cholesky_tiles))
    other_tiles = lax.ppermute(own_tiles, "dev", swap)
    partial = jnp.zeros((chips, vectors, points), jnp.float32)
    partial = add_terms(False, arrived, cholesky_tiles, partial)
    partial = add_terms(True, arrived, other_tiles, partial)
    returned = lax.all_to_all(
        partial, "dev", split_axis=0, concat_axis=0, tiled=True, axis_index_groups=same_core
    )
    return jnp.sum(returned, axis=0)


def solution(mesh):
    return jax.shard_map(
        local,
        mesh=mesh,
        in_specs=(P(None, "dev"), P("dev", None, None, None), P(), P("dev", None), P("dev")),
        out_specs=P(None, "dev"),
        check_vma=False,
    )
```

```python
import functools

import jax
import jax.numpy as jnp
from jax import lax
from jax.experimental import pallas as pl
from jax.experimental.pallas import tpu as pltpu
from jax.sharding import PartitionSpec as P

cores = 2
side = 4
per_owner = 2
capacity = cores * per_owner
sublanes = 8
id_rows = 16
chips_per_turn = 4
slots_per_turn = 8
sources_per_turn = 16


def swapped(place):
    across = place // (side * side)
    along = place // side % side
    return (along * side + across) * side + place % side


def pick_kernel(
    length_hbm,
    list_hbm,
    pairs_hbm,
    rows_hbm,
    out_hbm,
    rows,
    staged,
    length_ref,
    list_ref,
    pairs_ref,
    slots,
    fetch_sems,
    sems,
):
    edge = rows.shape[1]
    chips = staged.shape[0]
    owned = pairs_ref.shape[1] // (chips * cores)
    turns = chips // chips_per_turn
    length_fetch = pltpu.make_async_copy(length_hbm, length_ref, fetch_sems.at[0])
    list_fetch = pltpu.make_async_copy(list_hbm, list_ref, fetch_sems.at[1])
    pairs_fetch = pltpu.make_async_copy(pairs_hbm, pairs_ref, fetch_sems.at[2])
    fetch = pltpu.make_async_copy(rows_hbm, rows, fetch_sems.at[3])
    length_fetch.start()
    list_fetch.start()
    pairs_fetch.start()
    fetch.start()

    def clear(g, carry):
        for i in range(slots_per_turn):
            slots[g * slots_per_turn + i] = -1
        return carry

    lax.fori_loop(0, slots.shape[0] // slots_per_turn, clear, 0)
    length_fetch.wait()
    list_fetch.wait()

    def enter(s, carry):
        tile = list_ref[0, s]
        slot = tile // owned * per_owner
        slots[slot + jnp.where(slots[slot] >= 0, 1, 0)] = tile
        return carry

    def enter_group(g, carry):
        for i in range(slots_per_turn):
            enter(g * slots_per_turn + i, carry)
        return carry

    length = length_ref[0]
    groups = length // slots_per_turn
    lax.fori_loop(0, groups, enter_group, 0)
    lax.fori_loop(groups * slots_per_turn, length, enter, 0)
    pairs_fetch.wait()
    fetch.wait()
    lane = lax.broadcasted_iota(jnp.int32, (id_rows, edge), 1)

    def store(g):
        part = pl.ds(g * chips_per_turn, chips_per_turn)
        return pltpu.make_async_copy(staged.at[part], out_hbm.at[part], sems.at[g])

    def fill(g, carry):
        for i in range(chips_per_turn):
            place = g * chips_per_turn + i
            chip = swapped(place)
            ids = jnp.zeros((id_rows, edge), jnp.int32)
            for r in range(capacity):
                tile = slots[chip * capacity + r]
                known = jnp.maximum(tile, 0)
                for side in range(2):
                    at = (2 * r + side) * edge
                    staged[place, at : at + edge, :] = rows[pairs_ref[side, known]]
                ids = jnp.where(lane == r, jnp.where(tile >= 0, tile % owned + 1, 0), ids)
            top = 2 * capacity * edge
            staged[place, top : top + id_rows, :] = ids.astype(jnp.float32).astype(staged.dtype)
        store(g).start()
        return carry

    lax.fori_loop(0, turns, fill, 0)

    def finish(g, carry):
        store(g).wait()
        return carry

    lax.fori_loop(0, turns, finish, 0)


def pick_rows(length, entries, pairs, row_blocks, chips):
    blocks, edge, points = row_blocks.shape
    payload = 2 * capacity * edge + id_rows
    return pl.pallas_call(
        pick_kernel,
        out_shape=jax.ShapeDtypeStruct((chips, payload, points), row_blocks.dtype),
        in_specs=[pl.BlockSpec(memory_space=pl.ANY)] * 4,
        out_specs=pl.BlockSpec(memory_space=pl.ANY),
        scratch_shapes=[
            pltpu.VMEM((blocks, edge, points), row_blocks.dtype),
            pltpu.VMEM((chips, payload, points), row_blocks.dtype),
            pltpu.SMEM(length.shape, length.dtype),
            pltpu.SMEM(entries.shape, entries.dtype),
            pltpu.SMEM(pairs.shape, pairs.dtype),
            pltpu.SMEM((chips * capacity,), jnp.int32),
            pltpu.SemaphoreType.DMA((4,)),
            pltpu.SemaphoreType.DMA((chips // chips_per_turn,)),
        ],
        compiler_params=pltpu.CompilerParams(vmem_limit_bytes=56 * 2**20),
    )(length, entries, pairs, row_blocks)


def terms_kernel(partner, payload, tiles, before, out_ref, ids_row, ids):
    sources, _, points = payload.shape
    vectors, edge = tiles.shape[1:3]
    top = 2 * capacity * edge
    core = lax.rem(lax.axis_index("dev"), cores)
    first = (1 - core if partner else core) * per_owner
    for i in range(sources):
        row = payload[i, top : top + id_rows, :].astype(jnp.float32)[0:1, :]
        ids_row[i : i + 1, :] = row.astype(jnp.int32)
    pltpu.sync_copy(ids_row, ids)

    def one_turn(g, carry):
        for i in range(sources_per_turn):
            source = g * sources_per_turn + i
            total = jnp.zeros((vectors, sublanes, points), jnp.float32)
            for r in range(per_owner):
                slot = first + r
                found = ids[source, slot] - 1
                tile = tiles[jnp.maximum(found, 0)].reshape(vectors * edge, edge)
                at = pl.multiple_of(2 * slot * edge, edge)
                left = payload[source, pl.ds(at, edge), :].astype(jnp.float32)
                right = payload[source, pl.ds(at + edge, edge), :]
                product = jnp.dot(tile, right, preferred_element_type=jnp.float32)
                product = product.reshape(vectors, edge // sublanes, sublanes, points)
                left = left.reshape(1, edge // sublanes, sublanes, points)
                term = jnp.sum(product * left, axis=1)
                total = total + jnp.where(found >= 0, term, 0.0)
            out_ref[source] = before[source] + jnp.sum(total, axis=1)
        return carry

    lax.fori_loop(0, sources // sources_per_turn, one_turn, 0)


def add_terms(partner, payload, tiles, before):
    sources, rows, points = payload.shape
    return pl.pallas_call(
        functools.partial(terms_kernel, partner),
        out_shape=jax.ShapeDtypeStruct(before.shape, before.dtype),
        in_specs=[pl.BlockSpec(memory_space=pltpu.VMEM)] * 3,
        out_specs=pl.BlockSpec(memory_space=pltpu.VMEM),
        scratch_shapes=[
            pltpu.VMEM((sources, points), jnp.int32),
            pltpu.SMEM((sources, points), jnp.int32),
        ],
        compiler_params=pltpu.CompilerParams(vmem_limit_bytes=12 * 2**20),
        cost_estimate=pl.CostEstimate(
            flops=4 * sources * tiles.size // tiles.shape[0] * points,
            bytes_accessed=payload.size,
            transcendentals=0,
        ),
    )(payload, tiles, before)


def local(collocation, cholesky_tiles, tile_blocks, tile_lists, list_lengths):
    basis_count, points = collocation.shape
    vectors, edge = cholesky_tiles.shape[1:3]
    devices = lax.axis_size("dev")
    chips = devices // cores
    same_core = [[swapped(p) * cores + c for p in range(chips)] for c in range(cores)]
    swap = [(d, d ^ 1) for d in range(devices)]
    row_blocks = collocation.reshape(basis_count // edge, edge, points)
    sent = pick_rows(list_lengths, tile_lists, tile_blocks.T, row_blocks, chips)
    arrived = lax.all_to_all(
        sent, "dev", split_axis=0, concat_axis=0, tiled=True, axis_index_groups=same_core
    )
    _, own_tiles = lax.optimization_barrier((arrived, cholesky_tiles))
    other_tiles = lax.ppermute(own_tiles, "dev", swap)
    partial = jnp.zeros((chips, vectors, points), jnp.float32)
    partial = add_terms(False, arrived, cholesky_tiles, partial)
    partial = add_terms(True, arrived, other_tiles, partial)
    returned = lax.all_to_all(
        partial, "dev", split_axis=0, concat_axis=0, tiled=True, axis_index_groups=same_core
    )
    return jnp.sum(returned, axis=0)


def solution(mesh):
    return jax.shard_map(
        local,
        mesh=mesh,
        in_specs=(P(None, "dev"), P("dev", None, None, None), P(), P("dev", None), P("dev")),
        out_specs=P(None, "dev"),
        check_vma=False,
    )
```

```python
import functools

import jax
import jax.numpy as jnp
from jax import lax
from jax.experimental import pallas as pl
from jax.experimental.pallas import tpu as pltpu
from jax.sharding import PartitionSpec as P

cores = 2
side = 4
per_owner = 2
capacity = cores * per_owner
sublanes = 8
id_rows = 16
chips_per_turn = 4
slots_per_turn = 8
sources_per_turn = 16
slots_per_group = 32


def swapped(place):
    across = place // (side * side)
    along = place // side % side
    return (along * side + across) * side + place % side


def pick_kernel(
    length_hbm,
    list_hbm,
    pairs_hbm,
    rows_hbm,
    out_hbm,
    rows,
    staged,
    length_ref,
    list_ref,
    pairs_ref,
    slots,
    fetch_sems,
    sems,
):
    edge = rows.shape[1]
    chips = staged.shape[0]
    owned = pairs_ref.shape[1] // (chips * cores)
    turns = chips // chips_per_turn
    length_fetch = pltpu.make_async_copy(length_hbm, length_ref, fetch_sems.at[0])
    list_fetch = pltpu.make_async_copy(list_hbm, list_ref, fetch_sems.at[1])
    pairs_fetch = pltpu.make_async_copy(pairs_hbm, pairs_ref, fetch_sems.at[2])
    fetch = pltpu.make_async_copy(rows_hbm, rows, fetch_sems.at[3])
    length_fetch.start()
    list_fetch.start()
    pairs_fetch.start()
    fetch.start()

    def clear(g, carry):
        for i in range(slots_per_turn):
            slots[g * slots_per_turn + i] = -1
        return carry

    lax.fori_loop(0, slots.shape[0] // slots_per_turn, clear, 0)
    length_fetch.wait()
    list_fetch.wait()

    def enter(s, carry):
        tile = list_ref[0, s]
        slot = tile // owned * per_owner
        slots[slot + jnp.where(slots[slot] >= 0, 1, 0)] = tile
        return carry

    def enter_group(g, carry):
        for i in range(slots_per_turn):
            enter(g * slots_per_turn + i, carry)
        return carry

    length = length_ref[0]
    groups = length // slots_per_turn
    lax.fori_loop(0, groups, enter_group, 0)
    lax.fori_loop(groups * slots_per_turn, length, enter, 0)
    pairs_fetch.wait()
    fetch.wait()
    lane = lax.broadcasted_iota(jnp.int32, (id_rows, edge), 1)

    def store(g):
        part = pl.ds(g * chips_per_turn, chips_per_turn)
        return pltpu.make_async_copy(staged.at[part], out_hbm.at[part], sems.at[g])

    def fill(g, carry):
        for i in range(chips_per_turn):
            place = g * chips_per_turn + i
            chip = swapped(place)
            ids = jnp.zeros((id_rows, edge), jnp.int32)
            for r in range(capacity):
                tile = slots[chip * capacity + r]
                known = jnp.maximum(tile, 0)
                for side in range(2):
                    at = (2 * r + side) * edge
                    staged[place, at : at + edge, :] = rows[pairs_ref[side, known]]
                ids = jnp.where(lane == r, jnp.where(tile >= 0, tile % owned + 1, 0), ids)
            top = 2 * capacity * edge
            staged[place, top : top + id_rows, :] = ids.astype(jnp.float32).astype(staged.dtype)
        store(g).start()
        return carry

    lax.fori_loop(0, turns, fill, 0)

    def finish(g, carry):
        store(g).wait()
        return carry

    lax.fori_loop(0, turns, finish, 0)


def pick_rows(length, entries, pairs, row_blocks, chips):
    blocks, edge, points = row_blocks.shape
    payload = 2 * capacity * edge + id_rows
    return pl.pallas_call(
        pick_kernel,
        out_shape=jax.ShapeDtypeStruct((chips, payload, points), row_blocks.dtype),
        in_specs=[pl.BlockSpec(memory_space=pl.ANY)] * 4,
        out_specs=pl.BlockSpec(memory_space=pl.ANY),
        scratch_shapes=[
            pltpu.VMEM((blocks, edge, points), row_blocks.dtype),
            pltpu.VMEM((chips, payload, points), row_blocks.dtype),
            pltpu.SMEM(length.shape, length.dtype),
            pltpu.SMEM(entries.shape, entries.dtype),
            pltpu.SMEM(pairs.shape, pairs.dtype),
            pltpu.SMEM((chips * capacity,), jnp.int32),
            pltpu.SemaphoreType.DMA((4,)),
            pltpu.SemaphoreType.DMA((chips // chips_per_turn,)),
        ],
        compiler_params=pltpu.CompilerParams(vmem_limit_bytes=56 * 2**20),
    )(length, entries, pairs, row_blocks)


def terms_kernel(partner, payload, tiles, before, out_ref, ids_row, ids, live):
    sources, _, points = payload.shape
    vectors, edge = tiles.shape[1:3]
    top = 2 * capacity * edge
    core = lax.rem(lax.axis_index("dev"), cores)
    first = (1 - core if partner else core) * per_owner
    for i in range(sources):
        row = payload[i, top : top + id_rows, :].astype(jnp.float32)[0:1, :]
        ids_row[i : i + 1, :] = row.astype(jnp.int32)
    pltpu.sync_copy(ids_row, ids)
    out_ref[...] = before[...]

    def collect(g, count):
        for i in range(sources_per_turn):
            source = g * sources_per_turn + i
            for r in range(per_owner):
                live[count] = source * per_owner + r
                count = count + jnp.where(ids[source, first + r] > 0, 1, 0)
        return count

    count = lax.fori_loop(0, sources // sources_per_turn, collect, 0)

    def one_turn(g, carry):
        for i in range(slots_per_group):
            at_list = g * slots_per_group + i
            valid = at_list < count
            place = jnp.where(valid, live[at_list], 0)
            source = place // per_owner
            slot = first + place % per_owner
            tile = tiles[jnp.maximum(ids[source, slot] - 1, 0)].reshape(vectors * edge, edge)
            at = pl.multiple_of(2 * slot * edge, edge)
            left = payload[source, pl.ds(at, edge), :].astype(jnp.float32)
            right = payload[source, pl.ds(at + edge, edge), :]
            product = jnp.dot(tile, right, preferred_element_type=jnp.float32)
            product = product.reshape(vectors, edge // sublanes, sublanes, points)
            left = left.reshape(1, edge // sublanes, sublanes, points)
            term = jnp.sum(jnp.sum(product * left, axis=1), axis=1)
            out_ref[source] = out_ref[source] + jnp.where(valid, term, 0.0)
        return carry

    lax.fori_loop(0, (count + slots_per_group - 1) // slots_per_group, one_turn, 0)


def add_terms(partner, payload, tiles, before):
    sources, rows, points = payload.shape
    return pl.pallas_call(
        functools.partial(terms_kernel, partner),
        out_shape=jax.ShapeDtypeStruct(before.shape, before.dtype),
        in_specs=[pl.BlockSpec(memory_space=pltpu.VMEM)] * 3,
        out_specs=pl.BlockSpec(memory_space=pltpu.VMEM),
        scratch_shapes=[
            pltpu.VMEM((sources, points), jnp.int32),
            pltpu.SMEM((sources, points), jnp.int32),
            pltpu.SMEM((sources * per_owner + slots_per_group,), jnp.int32),
        ],
        compiler_params=pltpu.CompilerParams(vmem_limit_bytes=12 * 2**20),
        cost_estimate=pl.CostEstimate(
            flops=4 * sources * tiles.size // tiles.shape[0] * points,
            bytes_accessed=payload.size,
            transcendentals=0,
        ),
    )(payload, tiles, before)


def local(collocation, cholesky_tiles, tile_blocks, tile_lists, list_lengths):
    basis_count, points = collocation.shape
    vectors, edge = cholesky_tiles.shape[1:3]
    devices = lax.axis_size("dev")
    chips = devices // cores
    same_core = [[swapped(p) * cores + c for p in range(chips)] for c in range(cores)]
    swap = [(d, d ^ 1) for d in range(devices)]
    row_blocks = collocation.reshape(basis_count // edge, edge, points)
    sent = pick_rows(list_lengths, tile_lists, tile_blocks.T, row_blocks, chips)
    arrived = lax.all_to_all(
        sent, "dev", split_axis=0, concat_axis=0, tiled=True, axis_index_groups=same_core
    )
    _, own_tiles = lax.optimization_barrier((arrived, cholesky_tiles))
    other_tiles = lax.ppermute(own_tiles, "dev", swap)
    partial = jnp.zeros((chips, vectors, points), jnp.float32)
    partial = add_terms(False, arrived, cholesky_tiles, partial)
    partial = add_terms(True, arrived, other_tiles, partial)
    returned = lax.all_to_all(
        partial, "dev", split_axis=0, concat_axis=0, tiled=True, axis_index_groups=same_core
    )
    return jnp.sum(returned, axis=0)


def solution(mesh):
    return jax.shard_map(
        local,
        mesh=mesh,
        in_specs=(P(None, "dev"), P("dev", None, None, None), P(), P("dev", None), P("dev")),
        out_specs=P(None, "dev"),
        check_vma=False,
    )
```

```python
import functools

import jax
import jax.numpy as jnp
from jax import lax
from jax.experimental import pallas as pl
from jax.experimental.pallas import tpu as pltpu
from jax.sharding import PartitionSpec as P

cores = 2
side = 4
per_owner = 2
capacity = cores * per_owner
sublanes = 8
id_rows = 16
chips_per_turn = 4
slots_per_turn = 8
sources_per_turn = 16
slots_per_group = 32


def swapped(place):
    across = place // (side * side)
    along = place // side % side
    return (along * side + across) * side + place % side


def pick_kernel(
    length_hbm,
    list_hbm,
    pairs_hbm,
    rows_hbm,
    out_hbm,
    rows,
    staged,
    length_ref,
    list_ref,
    pairs_ref,
    slots,
    fetch_sems,
    sems,
):
    edge = rows.shape[1]
    chips = staged.shape[0]
    owned = pairs_ref.shape[1] // (chips * cores)
    turns = chips // chips_per_turn
    length_fetch = pltpu.make_async_copy(length_hbm, length_ref, fetch_sems.at[0])
    list_fetch = pltpu.make_async_copy(list_hbm, list_ref, fetch_sems.at[1])
    pairs_fetch = pltpu.make_async_copy(pairs_hbm, pairs_ref, fetch_sems.at[2])
    fetch = pltpu.make_async_copy(rows_hbm, rows, fetch_sems.at[3])
    length_fetch.start()
    list_fetch.start()
    pairs_fetch.start()
    fetch.start()

    def clear(g, carry):
        for i in range(slots_per_turn):
            slots[g * slots_per_turn + i] = -1
        return carry

    lax.fori_loop(0, slots.shape[0] // slots_per_turn, clear, 0)
    length_fetch.wait()
    list_fetch.wait()

    def enter(s, carry):
        tile = list_ref[0, s]
        slot = tile // owned * per_owner
        slots[slot + jnp.where(slots[slot] >= 0, 1, 0)] = tile
        return carry

    def enter_group(g, carry):
        for i in range(slots_per_turn):
            enter(g * slots_per_turn + i, carry)
        return carry

    length = length_ref[0]
    groups = length // slots_per_turn
    lax.fori_loop(0, groups, enter_group, 0)
    lax.fori_loop(groups * slots_per_turn, length, enter, 0)
    pairs_fetch.wait()
    fetch.wait()
    points = rows.shape[2]
    mine = swapped(lax.axis_index("dev") // cores)
    lane = lax.broadcasted_iota(jnp.int32, (id_rows, points), 1)
    lane = lane - mine % (points // capacity) * capacity

    def store(g):
        part = pl.ds(g * chips_per_turn, chips_per_turn)
        return pltpu.make_async_copy(staged.at[part], out_hbm.at[part], sems.at[g])

    def fill(g, carry):
        for i in range(chips_per_turn):
            place = g * chips_per_turn + i
            chip = swapped(place)
            ids = jnp.zeros((id_rows, points), jnp.int32)
            for r in range(capacity):
                tile = slots[chip * capacity + r]
                known = jnp.maximum(tile, 0)
                for side in range(2):
                    at = (2 * r + side) * edge
                    staged[place, at : at + edge, :] = rows[pairs_ref[side, known]]
                ids = jnp.where(lane == r, jnp.where(tile >= 0, tile % owned + 1, 0), ids)
            top = 2 * capacity * edge
            staged[place, top : top + id_rows, :] = ids.astype(jnp.float32).astype(staged.dtype)
        store(g).start()
        return carry

    lax.fori_loop(0, turns, fill, 0)

    def finish(g, carry):
        store(g).wait()
        return carry

    lax.fori_loop(0, turns, finish, 0)


def pick_rows(length, entries, pairs, row_blocks, chips):
    blocks, edge, points = row_blocks.shape
    payload = 2 * capacity * edge + id_rows
    return pl.pallas_call(
        pick_kernel,
        out_shape=jax.ShapeDtypeStruct((chips, payload, points), row_blocks.dtype),
        in_specs=[pl.BlockSpec(memory_space=pl.ANY)] * 4,
        out_specs=pl.BlockSpec(memory_space=pl.ANY),
        scratch_shapes=[
            pltpu.VMEM((blocks, edge, points), row_blocks.dtype),
            pltpu.VMEM((chips, payload, points), row_blocks.dtype),
            pltpu.SMEM(length.shape, length.dtype),
            pltpu.SMEM(entries.shape, entries.dtype),
            pltpu.SMEM(pairs.shape, pairs.dtype),
            pltpu.SMEM((chips * capacity,), jnp.int32),
            pltpu.SemaphoreType.DMA((4,)),
            pltpu.SemaphoreType.DMA((chips // chips_per_turn,)),
        ],
        compiler_params=pltpu.CompilerParams(vmem_limit_bytes=56 * 2**20),
    )(length, entries, pairs, row_blocks)


def terms_kernel(partner, payload, tiles, before, out_ref, ids_row, ids, live):
    sources, _, points = payload.shape
    vectors, edge = tiles.shape[1:3]
    top = 2 * capacity * edge
    core = lax.rem(lax.axis_index("dev"), cores)
    first = (1 - core if partner else core) * per_owner
    shared = points // capacity
    for h in range(sources // shared):
        row = jnp.zeros((id_rows, points), jnp.float32)
        for i in range(shared):
            row = row + payload[h * shared + i, top : top + id_rows, :].astype(jnp.float32)
        ids_row[h : h + 1, :] = row[0:1, :].astype(jnp.int32)
    pltpu.sync_copy(ids_row, ids)

    def id_of(source, slot):
        return ids[source // shared, source % shared * capacity + slot]

    out_ref[...] = before[...]

    def collect(g, count):
        for i in range(sources_per_turn):
            source = g * sources_per_turn + i
            for r in range(per_owner):
                live[count] = source * per_owner + r
                count = count + jnp.where(id_of(source, first + r) > 0, 1, 0)
        return count

    count = lax.fori_loop(0, sources // sources_per_turn, collect, 0)

    def one_turn(g, carry):
        for i in range(slots_per_group):
            at_list = g * slots_per_group + i
            valid = at_list < count
            place = jnp.where(valid, live[at_list], 0)
            source = place // per_owner
            slot = first + place % per_owner
            tile = tiles[jnp.maximum(id_of(source, slot) - 1, 0)].reshape(vectors * edge, edge)
            at = pl.multiple_of(2 * slot * edge, edge)
            left = payload[source, pl.ds(at, edge), :].astype(jnp.float32)
            right = payload[source, pl.ds(at + edge, edge), :]
            product = jnp.dot(tile, right, preferred_element_type=jnp.float32)
            product = product.reshape(vectors, edge // sublanes, sublanes, points)
            left = left.reshape(1, edge // sublanes, sublanes, points)
            term = jnp.sum(jnp.sum(product * left, axis=1), axis=1)
            out_ref[source] = out_ref[source] + jnp.where(valid, term, 0.0)
        return carry

    lax.fori_loop(0, (count + slots_per_group - 1) // slots_per_group, one_turn, 0)


def add_terms(partner, payload, tiles, before):
    sources, rows, points = payload.shape
    return pl.pallas_call(
        functools.partial(terms_kernel, partner),
        out_shape=jax.ShapeDtypeStruct(before.shape, before.dtype),
        in_specs=[pl.BlockSpec(memory_space=pltpu.VMEM)] * 3,
        out_specs=pl.BlockSpec(memory_space=pltpu.VMEM),
        scratch_shapes=[
            pltpu.VMEM((sublanes, points), jnp.int32),
            pltpu.SMEM((sublanes, points), jnp.int32),
            pltpu.SMEM((sources * per_owner + slots_per_group,), jnp.int32),
        ],
        compiler_params=pltpu.CompilerParams(vmem_limit_bytes=12 * 2**20),
        cost_estimate=pl.CostEstimate(
            flops=4 * sources * tiles.size // tiles.shape[0] * points,
            bytes_accessed=payload.size,
            transcendentals=0,
        ),
    )(payload, tiles, before)


def local(collocation, cholesky_tiles, tile_blocks, tile_lists, list_lengths):
    basis_count, points = collocation.shape
    vectors, edge = cholesky_tiles.shape[1:3]
    devices = lax.axis_size("dev")
    chips = devices // cores
    same_core = [[swapped(p) * cores + c for p in range(chips)] for c in range(cores)]
    swap = [(d, d ^ 1) for d in range(devices)]
    row_blocks = collocation.reshape(basis_count // edge, edge, points)
    sent = pick_rows(list_lengths, tile_lists, tile_blocks.T, row_blocks, chips)
    arrived = lax.all_to_all(
        sent, "dev", split_axis=0, concat_axis=0, tiled=True, axis_index_groups=same_core
    )
    _, own_tiles = lax.optimization_barrier((arrived, cholesky_tiles))
    other_tiles = lax.ppermute(own_tiles, "dev", swap)
    partial = jnp.zeros((chips, vectors, points), jnp.float32)
    partial = add_terms(False, arrived, cholesky_tiles, partial)
    partial = add_terms(True, arrived, other_tiles, partial)
    returned = lax.all_to_all(
        partial, "dev", split_axis=0, concat_axis=0, tiled=True, axis_index_groups=same_core
    )
    return jnp.sum(returned, axis=0)


def solution(mesh):
    return jax.shard_map(
        local,
        mesh=mesh,
        in_specs=(P(None, "dev"), P("dev", None, None, None), P(), P("dev", None), P("dev")),
        out_specs=P(None, "dev"),
        check_vma=False,
    )
```
